32 devices in a mesh: dp: 16 (over z, x, core), tensor: 2 (over y).
Axes of the slice: x: 2, y: 2, z: 4, core: 2. Of those that a mesh axis runs over, the one named last changes fastest.
Arguments:
- tokens: bfloat16 [32768, 1024], P(('dp', 'tensor')), may hold values from -6 to 6
- lengths: int32 [16, 4], P('dp'), may hold values from 1 to 1024, 2048 in all within a row
- cotangent: bfloat16 [32768, 1024], P(('dp', 'tensor')), may hold values from -6 to 6
- pre_gain: bfloat16 [1024], P(('dp', 'tensor')), may hold values from 0.099609375 to 1.8984375
- w_gate: bfloat16 [1024, 2048], P('dp', 'tensor'), may hold values from -0.1875 to 0.1875
- w_inner: bfloat16 [1024, 2048], P('dp', 'tensor'), may hold values from -0.1875 to 0.1875
- w_shared: bfloat16 [1024, 256], P(('dp', 'tensor')), may hold values from -0.1875 to 0.1875
- w_step: bfloat16 [1024, 32], P('dp', 'tensor'), may hold values from -0.1875 to 0.1875
- conv_inner: float32 [2048, 4], P('tensor'), may hold values from -3 to 3
- conv_inner_bias: float32 [2048], P('tensor'), may hold values from -0.5 to 0.5
- conv_shared: bfloat16 [256, 4], P(('dp', 'tensor')), may hold values from -3 to 3
- conv_shared_bias: bfloat16 [256], P(('dp', 'tensor')), may hold values from -0.5 to 0.5
- step_bias: float32 [32], P('tensor'), may hold values from -6 to -2
- decay_log: float32 [32], P('tensor'), may hold values from -4 to 1
- skip_gain: float32 [32], P('tensor'), may hold values from 0.5 to 1.5
- mix_gain: bfloat16 [2048], P('tensor'), may hold values from 0.099609375 to 1.8984375
- w_out: bfloat16 [2048, 1024], P('tensor', 'dp'), may hold values from -0.125 to 0.125
Outputs:
- output: bfloat16 [32768, 1024], P(('dp', 'tensor'))
- grad_tokens: float32 [32768, 1024], P(('dp', 'tensor'))
- grad_pre_gain: float32 [1024], P(('dp', 'tensor'))
- grad_w_gate: float32 [1024, 2048], P('dp', 'tensor')
- grad_w_inner: float32 [1024, 2048], P('dp', 'tensor')
- grad_w_shared: float32 [1024, 256], P(('dp', 'tensor'))
- grad_w_step: float32 [1024, 32], P('dp', 'tensor')
- grad_conv_inner: float32 [2048, 4], P('tensor')
- grad_conv_inner_bias: float32 [2048], P('tensor')
- grad_conv_shared: float32 [256, 4], P(('dp', 'tensor'))
- grad_conv_shared_bias: float32 [256], P(('dp', 'tensor'))
- grad_step_bias: float32 [32], P('tensor')
- grad_decay_log: float32 [32], P('tensor')
- grad_skip_gain: float32 [32], P('tensor')
- grad_mix_gain: float32 [2048], P('tensor')
- grad_w_out: float32 [2048, 1024], P('tensor', 'dp')
The draws below stay inside these ranges and needn't reach their ends.
Inputs may be any that keep to these rules, and one draw needn't show every extreme that they name: `lengths`: each row sums to 2048, and its longest sequence has exactly 1024 tokens.
All inputs are finite; a program needn't handle non-finite values.
Results may differ from the reference program's by a relative error of at most 0.014.
Values may be sent and summed in bfloat16 or wider, within the bound.
A program may use at most 384 MiB of HBM per device.

```python
import math
import jax
import jax.numpy as jnp
import numpy as np
from jax import lax

D = 1024
HEADS = 32
HEAD_DIM = 64
STATE = 128
CONV = 4
SCAN_BLOCK = 256
SLOTS = 4
INNER = 2048
GROUP = 2048
MOST = 1024
TOKENS = 32768
N_DP = 16


def block_levels(rng, shape, cuts, least, top_value):
    loudness, own = 1.0, jax.random.fold_in(rng, 6)
    for position, shards_of in cuts:
        steps = jnp.exp(jax.random.uniform(jax.random.fold_in(own, position), (shards_of,), jnp.float32, least / len(cuts), top_value / len(cuts)))
        loudness = loudness * jnp.repeat(steps, shape[position] // shards_of).reshape([-1 if axis == position else 1 for axis in range(len(shape))])
    return loudness


def profile(amount, total, reach, lean):
    portions = [(1 << 20) // math.isqrt(standing ** lean) + 1 for standing in range(2, amount + 1)]
    surplus, counts = total - reach - (amount - 1), [1] * (amount - 1)
    while surplus > 0:
        free = [i for i in range(amount - 1) if counts[i] < reach]
        pool, budget = sum([portions[i] for i in free]), surplus
        for i in free:
            more = min(reach - counts[i], max(1, budget * portions[i] // pool), surplus)
            counts[i] = counts[i] + more
            surplus = surplus - more
    return np.array([reach] + counts)


def uneven(stream_key, number_of, total, reach, skew):
    if number_of == 2:
        one = jax.random.randint(stream_key, (), max(1, total - reach), min(reach, total - 1) + 1)
        return jnp.stack([one, total - one])
    sizes = jnp.asarray(profile(number_of, total, reach, skew), jnp.int32)
    couples = (number_of - 1) // 2
    source_of, taker = sizes[1:1 + 2 * couples:2], sizes[2:2 + 2 * couples:2]
    margin = jnp.minimum(source_of - 1, reach - taker)
    moved = jax.random.randint(jax.random.fold_in(stream_key, 1), (couples,), 0, 1 << 20) % (margin + 1)
    sizes = sizes.at[1:1 + 2 * couples:2].set(source_of - moved).at[2:2 + 2 * couples:2].set(taker + moved)
    return sizes[jax.random.permutation(jax.random.fold_in(stream_key, 2), number_of)]


def centred(rng, extent, scale, reach, split=(), kind=jnp.bfloat16):
    values = jax.random.normal(rng, extent, jnp.float32) * scale
    if len(split) > 0:
        values = block_levels(rng, extent, split, -0.22, 0.18) * values
    return jnp.clip(values, min=-reach, max=reach).astype(kind)


def setup_inputs(seed: int = 0) -> dict:
    key_list = jax.random.split(jax.random.key(seed), 18)
    return {
        "tokens": centred(key_list[0], (TOKENS, D), 1.0, 6.0, ((0, 32),)),
        "lengths": jax.vmap(lambda own: uneven(own, SLOTS, GROUP, MOST, 2))(jax.random.split(key_list[1], N_DP)).reshape((N_DP, SLOTS)).astype(jnp.int32),
        "cotangent": centred(key_list[2], (TOKENS, D), 1.0, 6.0, ((0, 32),)),
        "pre_gain": jnp.clip(1.0 + 0.18 * jax.random.normal(key_list[3], (D,), jnp.float32), 0.099609375, 1.8984375).astype(jnp.bfloat16),
        "w_gate": centred(key_list[4], (D, INNER), D ** -0.5, 0.1875, ((0, 16), (1, 2))),
        "w_inner": centred(key_list[5], (D, INNER), D ** -0.5, 0.1875, ((0, 16), (1, 2))),
        "w_shared": centred(key_list[6], (D, 2 * STATE), D ** -0.5, 0.1875, ((0, 32),)),
        "w_step": centred(key_list[7], (D, HEADS), D ** -0.5, 0.1875, ((0, 16), (1, 2))),
        "conv_inner": centred(key_list[8], (INNER, CONV), 0.5, 3.0, ((0, 2),), jnp.float32),
        "conv_inner_bias": jnp.clip(jax.random.uniform(key_list[9], (INNER,), jnp.float32, -0.5, 0.5) * block_levels(key_list[9], (INNER,), ((0, 2),), -0.4, 0.0), -0.5, 0.5),
        "conv_shared": centred(key_list[10], (2 * STATE, CONV), 0.5, 3.0, ((0, 32),)),
        "conv_shared_bias": jnp.clip(jax.random.uniform(key_list[11], (2 * STATE,), jnp.float32, -0.5, 0.5) * block_levels(key_list[11], (2 * STATE,), ((0, 32),), -0.4, 0.0), -0.5, 0.5).astype(jnp.bfloat16),
        "step_bias": jnp.clip(-6.0 + 4.0 * jax.random.uniform(key_list[12], (HEADS,), jnp.float32) ** block_levels(key_list[12], (HEADS,), ((0, 2),), -0.2, 0.2), -6.0, -2.0),
        "decay_log": jnp.clip(-4.0 + 5.0 * jax.random.uniform(key_list[13], (HEADS,), jnp.float32) ** block_levels(key_list[13], (HEADS,), ((0, 2),), -0.2, 0.2), -4.0, 1.0),
        "skip_gain": jnp.clip(0.5 + 1.0 * jax.random.uniform(key_list[14], (HEADS,), jnp.float32) ** block_levels(key_list[14], (HEADS,), ((0, 2),), -0.2, 0.2), 0.5, 1.5),
        "mix_gain": jnp.clip(1.0 + 0.18 * jax.random.normal(key_list[15], (INNER,), jnp.float32), 0.099609375, 1.8984375).astype(jnp.bfloat16),
        "w_out": centred(key_list[16], (INNER, D), INNER ** -0.5, 0.125, ((0, 2), (1, 16))),
    }


@jax.custom_vjp
def low(v):
    return lax.optimization_barrier(v.astype(jnp.bfloat16)).astype(jnp.float32)

@jax.custom_vjp
def low_back(v):
    return v

def low_keep(v):
    return (low(v), None)

def low_pass(kept, grad):
    return (grad,)

def back_keep(v):
    return (v, None)

def back_low(kept, grad):
    return (low(grad),)
low.defvjp(low_keep, low_pass)
low_back.defvjp(back_keep, back_low)
EPS = 1e-05
HIGH = lax.Precision.HIGHEST

def segment_ids(lengths, count):
    ends = jnp.cumsum(lengths.astype(jnp.int32)).astype(jnp.int32)
    places = lax.broadcasted_iota(jnp.int32, (count, ends.shape[0]), 0)
    return lax.optimization_barrier(jnp.sum((places >= ends[None, :]).astype(jnp.int32), axis=1)).astype(jnp.int32)

def causal_conv(values, kernel, bias, seg):
    taps = kernel.shape[1]
    count = values.shape[0]
    padded = jnp.concatenate([jnp.zeros((taps - 1, values.shape[1]), values.dtype), values], axis=0)
    seg_pad = jnp.concatenate([jnp.full((taps - 1,), -1, jnp.int32), seg.astype(jnp.int32)])
    total = jnp.zeros_like(values) + bias[None, :]
    for place in range(taps):
        keep = (seg_pad[place:place + count] == seg).astype(values.dtype)
        total = total + kernel[:, place][None, :] * padded[place:place + count] * keep[:, None]
    return total

def block_terms(state, prev_seg, xs, step, decay, bmat, cmat, seg):
    kind = xs.dtype
    block = seg.shape[0]
    logs = jnp.cumsum(step * decay[None, :], axis=0)
    lower = lax.broadcasted_iota(jnp.int32, (block, block), 0) >= lax.broadcasted_iota(jnp.int32, (block, block), 1)
    same = (seg[:, None] == seg[None, :]) & lower
    diff = logs[:, None, :] - logs[None, :, :]
    weights = jnp.exp(jnp.where(same[:, :, None], diff, -10000.0))
    scores = jnp.dot(cmat, bmat.T, precision=HIGH)
    weighted = scores[:, :, None] * weights * step[None, :, :]
    inner = jnp.einsum('ijh,jhp->ihp', weighted, xs, precision=HIGH)
    carried = (seg == prev_seg).astype(kind)[:, None] * jnp.exp(logs)
    inner = inner + carried[:, :, None] * jnp.einsum('in,hnp->ihp', cmat, state, precision=HIGH)
    tail = jnp.exp(logs[-1][None, :] - logs) * (seg == seg[-1]).astype(kind)[:, None] * step
    new_state = carried[-1][:, None, None] * state + jnp.einsum('jh,jn,jhp->hnp', tail, bmat, xs, precision=HIGH)
    return (new_state, inner)

def scan_group(xs, step, decay, bmat, cmat, seg):
    count, heads, width = xs.shape
    states = bmat.shape[1]
    blocks = count // SCAN_BLOCK

    def advance(carry, pieces):
        state, prev = carry
        piece_x, piece_step, piece_b, piece_c, piece_seg = pieces
        new_state, out = jax.checkpoint(block_terms)(state, prev, piece_x, piece_step, decay, piece_b, piece_c, piece_seg)
        return ((new_state, piece_seg[-1]), out)
    init = (jnp.zeros((heads, states, width), xs.dtype), jnp.array(-1, jnp.int32))
    pieces = (xs.reshape(blocks, SCAN_BLOCK, heads, width), step.reshape(blocks, SCAN_BLOCK, heads), bmat.reshape(blocks, SCAN_BLOCK, states), cmat.reshape(blocks, SCAN_BLOCK, states), seg.reshape(blocks, SCAN_BLOCK))
    _, outs = lax.scan(advance, init, pieces)
    return outs.reshape(count, heads, width)

def group_forward(params, rows, lengths):
    pre_gain, w_gate, w_inner, w_shared, w_step, conv_inner, conv_inner_bias, conv_shared, conv_shared_bias, step_bias, decay_log, skip_gain, mix_gain, w_out = params
    count = rows.shape[0]
    seg = segment_ids(lengths, count)
    rinv = lax.rsqrt(lax.optimization_barrier(jnp.mean(rows * rows, axis=-1, keepdims=True)) + EPS)
    normed_in = low(rows * rinv * pre_gain[None, :])
    gate = low_back(jnp.dot(normed_in, w_gate, precision=HIGH))
    inner_pre = low_back(jnp.dot(normed_in, w_inner, precision=HIGH))
    shared_pre = low_back(jnp.dot(normed_in, w_shared, precision=HIGH))
    step_raw = low_back(jnp.dot(normed_in, w_step, precision=HIGH))
    inner_conv = jax.nn.silu(causal_conv(inner_pre, conv_inner, conv_inner_bias, seg))
    shared_conv = jax.nn.silu(causal_conv(shared_pre, conv_shared, conv_shared_bias, seg))
    step = jax.nn.softplus(step_raw + step_bias[None, :])
    decay = -jnp.exp(decay_log)
    heads_in = inner_conv.reshape(count, HEADS, HEAD_DIM)
    scan_out = scan_group(heads_in, step, decay, shared_conv[:, :STATE], shared_conv[:, STATE:], seg)
    scan_out = scan_out + skip_gain[None, :, None] * heads_in
    gated = scan_out.reshape(count, INNER) * jax.nn.silu(gate)
    rmix = lax.rsqrt(lax.optimization_barrier(jnp.mean(gated * gated, axis=-1, keepdims=True)) + EPS)
    mixed = low(gated * rmix * mix_gain[None, :])
    return rows + jnp.dot(mixed, w_out, precision=HIGH)

def reference(tokens, lengths, cotangent, pre_gain, w_gate, w_inner, w_shared, w_step, conv_inner, conv_inner_bias, conv_shared, conv_shared_bias, step_bias, decay_log, skip_gain, mix_gain, w_out):
    params = tuple((item.astype(jnp.float32) for item in (pre_gain, w_gate, w_inner, w_shared, w_step, conv_inner, conv_inner_bias, conv_shared, conv_shared_bias, step_bias, decay_log, skip_gain, mix_gain, w_out)))
    rows = tokens.astype(jnp.float32).reshape(N_DP, GROUP, D)

    def forward(weights, inputs):
        return lax.map(lambda item: jax.checkpoint(group_forward)(weights, item[0], item[1]), (inputs, lengths))
    result, pull = jax.vjp(forward, params, rows)
    grads, grad_rows = pull(cotangent.astype(jnp.float32).reshape(N_DP, GROUP, D))
    return (result.reshape(TOKENS, D).astype(jnp.bfloat16), grad_rows.reshape(TOKENS, D), grads[0], grads[1], grads[2], grads[3], grads[4], grads[5], grads[6], grads[7], grads[8], grads[9], grads[10], grads[11], grads[12], grads[13])
```

```python
import functools

import jax
import jax.numpy as jnp
from jax import lax
from jax.experimental import pallas as pl
from jax.experimental.pallas import tpu as pltpu
from jax.sharding import PartitionSpec as P

EPS = 1e-05
HIGH = lax.Precision.HIGHEST
Q = 128
LANES = 128
F32 = jnp.float32
BF16 = jnp.bfloat16
LAST = (((1,), (1,)), ((), ()))
FIRST = (((0,), (0,)), ((), ()))
VMEM_LIMIT = 56 * 1024 * 1024


def segment_ids(lengths, count):
    ends = jnp.cumsum(lengths)
    places = lax.broadcasted_iota(jnp.int32, (count, ends.shape[0]), 0)
    return jnp.sum((places >= ends[None, :]).astype(jnp.int32), axis=1)


def contract_last(left, right):
    return lax.dot_general(left, right, LAST, preferred_element_type=F32)


def contract_first(left, right):
    return lax.dot_general(left, right, FIRST, preferred_element_type=F32)


def mul(left, right):
    return jnp.dot(left, right, preferred_element_type=F32)


def halves(value):
    high = value.astype(BF16)
    return high, (value - high.astype(F32)).astype(BF16)


def spread(value, expand):
    high, low = halves(value)
    return mul(high, expand) + mul(low, expand)


def per_head(value, expand):
    high, low = halves(value)
    return contract_last(high, expand) + contract_last(low, expand)


def shifted(value, halo, cols):
    ext = jnp.concatenate([halo, value], axis=0)
    return [pltpu.roll(ext, s, axis=0)[8:] * cols[:, s : s + 1] for s in (1, 2, 3)]


def convolve(value, earlier, taps):
    total = taps[4:5] + taps[3:4] * value
    for s in (1, 2, 3):
        total = total + taps[3 - s : 4 - s] * earlier[s - 1]
    return total


def convolve_back(grad, later, cols, taps):
    ext = jnp.concatenate([grad, later], axis=0)
    count = grad.shape[0]
    total = taps[3:4] * grad
    for s in (1, 2, 3):
        moved = pltpu.roll(ext, count + 8 - s, axis=0)[:count]
        total = total + taps[3 - s : 4 - s] * (moved * cols[:, 5 + s : 6 + s])
    return total


def tap_grads(grad, value, earlier):
    rows = [jnp.sum(grad * earlier[2 - k], axis=0, keepdims=True) for k in range(3)]
    rows.append(jnp.sum(grad * value, axis=0, keepdims=True))
    rows.append(jnp.sum(grad, axis=0, keepdims=True))
    return rows


def block_terms(pre_ref, halo_ref, sh_ref, halo_sh_ref, step_ref, rate_ref, rate_row_ref, cols, seg_row_ref, ti, ts, expand):
    pre, sh = pre_ref[...], sh_ref[...]
    near, near_s = shifted(pre, halo_ref[...], cols), shifted(sh, halo_sh_ref[...], cols)
    z, zs = convolve(pre, near, ti), convolve(sh, near_s, ts)
    rows = lax.broadcasted_iota(jnp.int32, (Q, Q), 0)
    lanes = lax.broadcasted_iota(jnp.int32, (Q, Q), 1)
    lower = (rows >= lanes).astype(F32)
    upper = (rows <= lanes).astype(F32)
    logs = jnp.dot(lower, rate_ref[...], precision=HIGH, preferred_element_type=F32)
    logs_row = jnp.dot(rate_row_ref[...], upper, precision=HIGH, preferred_element_type=F32)
    step_e = spread(step_ref[...], expand)
    carried = spread(jnp.exp(logs) * cols[:, 4:5], expand)
    tail = spread(jnp.exp(logs[Q - 1 : Q] - logs) * cols[:, 5:6], expand)
    mask = (cols[:, 0:1] == seg_row_ref[0:1, :]) & (rows >= lanes)
    return pre, sh, near, near_s, z, zs, logs, logs_row, step_e, carried, tail, mask


def decays(logs, logs_row, mask, h):
    diff = logs[:, h : h + 1] - logs_row[h : h + 1, :]
    return jnp.exp(jnp.where(mask, diff, -10000.0))


def forward_kernel(
    heads, pre_ref, halo_ref, gate_ref, sh_ref, halo_sh_ref, step_ref, rate_ref, rate_row_ref,
    cols_ref, seg_row_ref, ti_ref, ts_ref, expand_ref, gated_ref, states_ref, sums_ref, state,
):
    @pl.when(pl.program_id(0) == 0)
    def _():
        state[...] = jnp.zeros_like(state)

    cols, ti, ts, expand = cols_ref[...], ti_ref[...], ts_ref[...], expand_ref[...]
    _, _, _, _, z, zs, logs, logs_row, step_e, carried, tail, mask = block_terms(
        pre_ref, halo_ref, sh_ref, halo_sh_ref, step_ref, rate_ref, rate_row_ref, cols, seg_row_ref, ti, ts, expand
    )
    x = z * jax.nn.sigmoid(z)
    shared = (zs * jax.nn.sigmoid(zs)).astype(BF16)
    b, c = shared[:, :LANES], shared[:, LANES:]
    xs = step_e * x
    low_lanes = ti[7:8]
    x_even = (xs * low_lanes).astype(BF16)
    x_odd = (xs * (1.0 - low_lanes)).astype(BF16)
    entering = state[...]
    entering_low = entering.astype(BF16)
    states_ref[...] = entering_low
    scores = contract_last(c, b)
    base = carried * mul(c, entering_low) + ti[5:6] * x
    state[...] = carried[Q - 1 : Q] * entering + contract_first(b, (tail * xs).astype(BF16))
    total = jnp.zeros((Q, LANES), F32)
    for pair in range(heads // 2):
        at = slice(pair * LANES, (pair + 1) * LANES)
        both = jnp.concatenate(
            [scores * decays(logs, logs_row, mask, 2 * pair + i) for i in range(2)], axis=1
        ).astype(BF16)
        y = base[:, at] + mul(both, jnp.concatenate([x_even[:, at], x_odd[:, at]], axis=0))
        gate = gate_ref[:, at]
        gated = y * (gate * jax.nn.sigmoid(gate))
        gated_ref[:, at] = gated
        total = total + gated * gated
    sums_ref[...] = jnp.broadcast_to(jnp.sum(total, axis=1, keepdims=True), (Q, LANES))


def backward_kernel(
    heads, pre_ref, halo_ref, gate_ref, sh_ref, halo_sh_ref, step_ref, rate_ref, rate_row_ref,
    cols_ref, seg_row_ref, ti_ref, ts_ref, expand_ref, states_ref, gm_ref, gated_ref, norms_ref,
    low_ref, dsh_ref, dstep_ref, dlog_ref, dlog_row_ref, acc_i_ref, acc_s_ref,
    dstate, later, later_s,
):
    @pl.when(pl.program_id(0) == 0)
    def _():
        dstate[...] = jnp.zeros_like(dstate)
        later[...] = jnp.zeros_like(later)
        later_s[...] = jnp.zeros_like(later_s)
        acc_i_ref[...] = jnp.zeros_like(acc_i_ref)
        acc_s_ref[...] = jnp.zeros_like(acc_s_ref)

    width = pre_ref.shape[1]
    cols, ti, ts, expand = cols_ref[...], ti_ref[...], ts_ref[...], expand_ref[...]
    pre, sh, near, near_s, z, zs, logs, logs_row, step_e, carried, tail, mask = block_terms(
        pre_ref, halo_ref, sh_ref, halo_sh_ref, step_ref, rate_ref, rate_row_ref, cols, seg_row_ref, ti, ts, expand
    )
    sig, sig_s = jax.nn.sigmoid(z), jax.nn.sigmoid(zs)
    x = z * sig
    shared = (zs * sig_s).astype(BF16)
    b, c = shared[:, :LANES], shared[:, LANES:]
    xs = step_e * x
    low_lanes = ti[7:8]
    high_lanes = 1.0 - low_lanes
    x_low = xs.astype(BF16)
    x_even = (xs * low_lanes).astype(BF16)
    x_odd = (xs * high_lanes).astype(BF16)
    skip = ti[5:6]

    gm, gated, gate, norms = gm_ref[...], gated_ref[...], gate_ref[...], norms_ref[...]
    rmix, pull = norms[:, 0:1], norms[:, 1:2]
    dgated = gm * ti[6:7] * rmix - gated * pull
    dgain = jnp.sum(gm * gated * rmix, axis=0, keepdims=True)
    sig_g = jax.nn.sigmoid(gate)
    dy = dgated * (gate * sig_g)
    dgate_scale = dgated * (sig_g * (1.0 + gate * (1.0 - sig_g)))
    dy_even = (dy * low_lanes).astype(BF16)
    dy_odd = (dy * high_lanes).astype(BF16)

    entering = states_ref[...]
    leaving = dstate[...]
    leaving_low = leaving.astype(BF16)
    scores = contract_last(c, b)
    from_state = carried * mul(c, entering)
    base = from_state + skip * x
    carried_dy = carried * dy
    carried_low = carried_dy.astype(BF16)
    tail_x = tail * xs
    tail_low = tail_x.astype(BF16)
    reach = mul(b, leaving_low)
    last_row = carried[Q - 1 : Q]
    pulled = jnp.sum(entering.astype(F32) * leaving, axis=0, keepdims=True) * last_row
    dstate[...] = last_row * leaving + contract_first(c, carried_low)

    lane = lax.broadcasted_iota(jnp.int32, (Q, LANES), 1)
    dscores = jnp.zeros((Q, Q), F32)
    row_sums = jnp.zeros((Q, LANES), F32)
    col_sums = []
    grads = []
    for pair in range(heads // 2):
        at = slice(pair * LANES, (pair + 1) * LANES)
        weights = [decays(logs, logs_row, mask, 2 * pair + i) for i in range(2)]
        mats = [(scores * w).astype(BF16) for w in weights]
        y = base[:, at] + mul(
            jnp.concatenate(mats, axis=1), jnp.concatenate([x_even[:, at], x_odd[:, at]], axis=0)
        )
        low_ref[:, at] = (dgate_scale[:, at] * y).astype(BF16)
        dys = jnp.concatenate([dy_even[:, at], dy_odd[:, at]], axis=0)
        cross = contract_last(dys, x_low[:, at])
        for i in range(2):
            part = cross[i * Q : (i + 1) * Q] * weights[i]
            dscores = dscores + part
            part = part * scores
            h = 2 * pair + i
            row_sums = jnp.where(lane == h, jnp.sum(part, axis=1, keepdims=True), row_sums)
            col_sums.append(jnp.sum(part, axis=0, keepdims=True))
        grads.append(contract_first(jnp.concatenate(mats, axis=0), dys))
    spare = dlog_row_ref.shape[0] - heads
    if spare:
        col_sums.append(jnp.zeros((spare, Q), F32))
    dlog_row_ref[...] = jnp.concatenate(col_sums, axis=0)
    dxs = jnp.concatenate(grads, axis=1) + tail * reach

    tail_term = tail_x * reach
    at_end = pulled + jnp.sum(tail_term, axis=0, keepdims=True)
    ends = lax.broadcasted_iota(jnp.int32, (Q, width), 0) == Q - 1
    log_term = dy * from_state - tail_term + jnp.where(ends, at_end, 0.0)
    dlog_ref[...] = row_sums + per_head(log_term, expand)
    dstep_ref[...] = per_head(x * dxs, expand)

    dx = step_e * dxs + skip * dy
    dz = dx * (sig * (1.0 + z * (1.0 - sig)))
    low_ref[:, width:] = convolve_back(dz, later[...], cols, ti).astype(BF16)
    later[...] = dz[:8]
    rows = tap_grads(dz, pre, near)
    rows += [jnp.sum(dy * x, axis=0, keepdims=True), dgain, jnp.zeros((1, width), F32)]
    acc_i_ref[...] += jnp.concatenate(rows, axis=0)

    dlow = dscores.astype(BF16)
    dc = mul(dlow, b) + contract_last(carried_low, entering)
    db = contract_first(dlow, c) + contract_last(tail_low, leaving_low)
    dzs = jnp.concatenate([db, dc], axis=1) * (sig_s * (1.0 + zs * (1.0 - sig_s)))
    dsh_ref[...] = convolve_back(dzs, later_s[...], cols, ts)
    later_s[...] = dzs[:8]
    rows = tap_grads(dzs, sh, near_s) + [jnp.zeros((3, dzs.shape[1]), F32)]
    acc_s_ref[...] += jnp.concatenate(rows, axis=0)


def block_specs(width, shared_width, row_heads, blocks, place):
    def halo(k):
        return jnp.maximum(place(k) * (Q // 8) - 1, 0)

    return [
        pl.BlockSpec((Q, width), lambda k: (place(k), 1)),
        pl.BlockSpec((8, width), lambda k: (halo(k), 1)),
        pl.BlockSpec((Q, width), lambda k: (place(k), 0)),
        pl.BlockSpec((Q, shared_width), lambda k: (place(k), 0)),
        pl.BlockSpec((8, shared_width), lambda k: (halo(k), 0)),
        pl.BlockSpec((Q, LANES), lambda k: (place(k), 0)),
        pl.BlockSpec((Q, LANES), lambda k: (place(k), 0)),
        pl.BlockSpec((row_heads, Q), lambda k: (0, place(k))),
        pl.BlockSpec((Q, LANES), lambda k: (place(k), 0)),
        pl.BlockSpec((8, Q), lambda k: (0, place(k))),
        pl.BlockSpec((8, width), lambda k: (0, 0)),
        pl.BlockSpec((8, shared_width), lambda k: (0, 0)),
        pl.BlockSpec((LANES, width), lambda k: (0, 0)),
    ]


def mixer_forward(heads, width, args):
    proj, shared = args[0], args[3]
    count, shared_width, row_heads = proj.shape[0], shared.shape[1], args[7].shape[0]
    blocks = count // Q
    return pl.pallas_call(
        functools.partial(forward_kernel, heads),
        grid=(blocks,),
        in_specs=block_specs(width, shared_width, row_heads, blocks, lambda k: k),
        out_specs=[
            pl.BlockSpec((Q, width), lambda k: (k, 0)),
            pl.BlockSpec((LANES, width), lambda k: (k, 0)),
            pl.BlockSpec((Q, LANES), lambda k: (k, 0)),
        ],
        out_shape=[
            jax.ShapeDtypeStruct((count, width), F32),
            jax.ShapeDtypeStruct((blocks * LANES, width), BF16),
            jax.ShapeDtypeStruct((count, LANES), F32),
        ],
        scratch_shapes=[pltpu.VMEM((LANES, width), F32)],
        compiler_params=pltpu.CompilerParams(vmem_limit_bytes=VMEM_LIMIT),
        cost_estimate=pl.CostEstimate(flops=count * width * 1500, bytes_accessed=count * width * 14, transcendentals=count * width * 4),
    )(*args)


def mixer_backward(heads, width, args):
    proj, shared = args[0], args[3]
    count, shared_width, row_heads = proj.shape[0], shared.shape[1], args[7].shape[0]
    blocks = count // Q
    here = lambda k: blocks - 1 - k
    rows = lambda k: (here(k), 0)
    return pl.pallas_call(
        functools.partial(backward_kernel, heads),
        grid=(blocks,),
        in_specs=block_specs(width, shared_width, row_heads, blocks, here)
        + [
            pl.BlockSpec((LANES, width), rows),
            pl.BlockSpec((Q, width), rows),
            pl.BlockSpec((Q, width), rows),
            pl.BlockSpec((Q, LANES), rows),
        ],
        out_specs=[
            pl.BlockSpec((Q, 2 * width), rows),
            pl.BlockSpec((Q, shared_width), rows),
            pl.BlockSpec((Q, LANES), rows),
            pl.BlockSpec((Q, LANES), rows),
            pl.BlockSpec((row_heads, Q), lambda k: (0, here(k))),
            pl.BlockSpec((8, width), lambda k: (0, 0)),
            pl.BlockSpec((8, shared_width), lambda k: (0, 0)),
        ],
        out_shape=[
            jax.ShapeDtypeStruct((count, 2 * width), BF16),
            jax.ShapeDtypeStruct((count, shared_width), F32),
            jax.ShapeDtypeStruct((count, LANES), F32),
            jax.ShapeDtypeStruct((count, LANES), F32),
            jax.ShapeDtypeStruct((row_heads, count), F32),
            jax.ShapeDtypeStruct((8, width), F32),
            jax.ShapeDtypeStruct((8, shared_width), F32),
        ],
        scratch_shapes=[
            pltpu.VMEM((LANES, width), F32),
            pltpu.VMEM((8, width), F32),
            pltpu.VMEM((8, shared_width), F32),
        ],
        compiler_params=pltpu.CompilerParams(vmem_limit_bytes=VMEM_LIMIT),
        cost_estimate=pl.CostEstimate(flops=count * width * 4000, bytes_accessed=count * width * 24, transcendentals=count * width * 5),
    )(*args)


def pad_lanes(value, lanes=LANES):
    return jnp.pad(value, ((0, 0), (0, lanes - value.shape[1])))


def token_columns(seg, heads):
    count = seg.shape[0]
    early = [jnp.concatenate([jnp.full((s,), -1, jnp.int32), seg[:-s]]) == seg for s in (1, 2, 3)]
    late = [jnp.concatenate([seg[s:], jnp.full((s,), -1, jnp.int32)]) == seg for s in (1, 2, 3)]
    by_block = seg.reshape(count // Q, Q)
    prev = jnp.concatenate([jnp.full((1,), -1, jnp.int32), by_block[:-1, -1]])
    enters = (by_block == prev[:, None]).reshape(count)
    leaves = (by_block == by_block[:, -1:]).reshape(count)
    stack = [seg] + early + [enters, leaves] + late
    return pad_lanes(jnp.stack([v.astype(F32) for v in stack], axis=1))


def shards(
    tokens, lengths, cotangent, pre_gain, w_gate, w_inner, w_shared, w_step, conv_inner,
    conv_inner_bias, conv_shared, conv_shared_bias, step_bias, decay_log, skip_gain, mix_gain, w_out,
):
    tensor_count, dp_count = lax.axis_size("tensor"), lax.axis_size("dp")
    everyone = tensor_count * dp_count
    rows_dev, width = tokens.shape
    group = rows_dev * tensor_count
    heads = step_bias.shape[0]
    inner = w_gate.shape[1]
    head_width = inner // heads
    shared_width = w_shared.shape[1]
    inner_all = inner * tensor_count
    row_heads = -(-heads // 8) * 8

    own_w, own_g, own_c = w_shared.shape[0], pre_gain.shape[0], conv_shared.shape[0]
    taps = conv_shared.shape[1]
    extra = jnp.concatenate([pre_gain, conv_shared.reshape(-1), conv_shared_bias])
    extra = jnp.pad(extra, (0, shared_width - extra.shape[0]))[None, :]
    packed_rows = -(-(own_w + 1) // 16) * 16
    packed = jnp.concatenate([w_shared, extra], axis=0)
    packed = jnp.pad(packed, ((0, packed_rows - own_w - 1), (0, 0)))
    packed = lax.all_gather(packed, ("dp", "tensor"), axis=0, tiled=False)
    shared_full = packed[:, :own_w].reshape(width, shared_width)
    extras = packed[:, own_w]
    gain_full = extras[:, :own_g].reshape(-1)
    kernel_shared = extras[:, own_g : own_g + own_c * taps].reshape(shared_width, taps)
    bias_shared = extras[:, own_g + own_c * taps : own_g + own_c * taps + own_c].reshape(-1)

    split_full = lax.all_gather(
        jnp.concatenate([w_gate, w_inner, pad_lanes(w_step)], axis=1), "dp", axis=0, tiled=True
    )
    out_full = lax.all_gather(w_out.T, "dp", axis=0, tiled=True)
    cot_all = lax.all_gather(cotangent, "tensor", axis=0, tiled=True)

    rows = tokens.astype(F32)
    gain_pre = gain_full.astype(F32)[None, :]
    rinv = lax.rsqrt(jnp.mean(rows * rows, axis=-1, keepdims=True) + EPS)
    normed_in = (rows * rinv * gain_pre).astype(BF16)
    gathered = lax.all_gather(normed_in, "tensor", axis=0, tiled=True)
    proj = mul(gathered, split_full[:, : 2 * inner])
    step_raw = mul(gathered, split_full[:, 2 * inner :])[:, :heads]
    shared_pre = mul(gathered, shared_full)
    seg = segment_ids(lengths[0], group)

    shifted_step = step_raw + step_bias[None, :]
    step = jax.nn.softplus(shifted_step)
    decay = -jnp.exp(decay_log)
    rate = step * decay[None, :]
    rate_row = jnp.pad(rate.T, ((0, row_heads - heads), (0, 0)))
    cols = token_columns(seg, heads)
    seg_row = jnp.broadcast_to(seg.astype(F32)[None, :], (8, group))
    channel = jnp.arange(inner)
    low_lanes = (channel % LANES < head_width).astype(F32)
    gain_mix = mix_gain.astype(F32)
    taps_inner = jnp.concatenate(
        [conv_inner.T, jnp.stack([conv_inner_bias, jnp.repeat(skip_gain, head_width), gain_mix, low_lanes])]
    )
    taps_shared = jnp.pad(
        jnp.concatenate([kernel_shared.T, bias_shared[None, :]]).astype(F32), ((0, 7 - taps), (0, 0))
    )
    expand = (jnp.arange(LANES)[:, None] == channel[None, :] // head_width).astype(BF16)
    args = (
        proj, proj, proj, shared_pre, shared_pre, pad_lanes(step), pad_lanes(rate), rate_row,
        cols, seg_row, taps_inner, taps_shared, expand,
    )
    gated, states, sums = mixer_forward(heads, inner, args)

    grad_mixed = mul(cot_all, out_full)
    crosses = jnp.sum(grad_mixed * gain_mix[None, :] * gated, axis=-1)
    square_sum, cross = lax.psum(jnp.stack([sums[:, 0], crosses]), "tensor")
    rmix = lax.rsqrt(square_sum / inner_all + EPS)
    mixed = (gated * rmix[:, None] * gain_mix[None, :]).astype(BF16)
    out_term = contract_first(cot_all, mixed).astype(BF16)
    owned_out = lax.psum_scatter(out_term, "dp", scatter_dimension=0, tiled=True).astype(F32).T
    partial_value = contract_last(mixed, out_full)
    out_rows = lax.psum_scatter(partial_value, "tensor", scatter_dimension=0, tiled=True)
    output = (rows + out_rows).astype(BF16)

    norms = pad_lanes(jnp.stack([rmix, rmix**3 * cross / inner_all], axis=1))
    low, d_shared, d_step_part, d_log, d_log_row, acc_inner, acc_shared = mixer_backward(
        heads, inner, args + (states, grad_mixed, gated, norms)
    )
    d_logs = (d_log[:, :heads] - d_log_row[:heads].T).reshape(group // Q, Q, heads)
    after = (jnp.arange(Q)[:, None] <= jnp.arange(Q)[None, :]).astype(F32)
    d_rate = jnp.einsum("ti,kih->kth", after, d_logs, precision=HIGH).reshape(group, heads)
    d_step = (d_step_part[:, :heads] + d_rate * decay[None, :]) * jax.nn.sigmoid(shifted_step)
    d_decay = jnp.sum(d_rate * step, axis=0) * decay
    step_low = pad_lanes(d_step.astype(BF16))

    back_part = contract_last(low, split_full[:, : 2 * inner]) + contract_last(
        step_low, split_full[:, 2 * inner :]
    )
    split_grad = jnp.concatenate(
        [contract_first(gathered, low).astype(BF16), contract_first(gathered, step_low).astype(BF16)], axis=1
    )
    owned_split = lax.psum_scatter(split_grad, "dp", scatter_dimension=0, tiled=True).astype(F32)
    back_rows = lax.psum_scatter(
        jnp.concatenate([back_part, d_shared], axis=1), "tensor", scatter_dimension=0, tiled=True
    )
    shared_low = back_rows[:, width:].astype(BF16)
    back_rows = back_rows[:, :width] + contract_last(shared_low, shared_full)
    grad_shared_w = contract_first(normed_in, shared_low)
    grad_pre = jnp.sum(back_rows * rows * rinv, axis=0)
    upstream_pre = back_rows * gain_pre
    grad_tokens = (
        upstream_pre * rinv
        - rows * rinv**3 * jnp.sum(upstream_pre * rows, axis=-1, keepdims=True) / width
        + cotangent.astype(F32)
    )
    tail = jnp.concatenate(
        [
            grad_pre.reshape(everyone, own_g),
            acc_shared[:taps].T.reshape(everyone, own_c * taps),
            acc_shared[taps].reshape(everyone, own_c),
        ],
        axis=1,
    )
    tail = pad_lanes(tail, shared_width)[:, None, :]
    back_rows_dev = -(-(own_w + 1) // 8) * 8
    give = jnp.concatenate([grad_shared_w.reshape(everyone, own_w, shared_width), tail], axis=1)
    give = jnp.pad(give, ((0, 0), (0, back_rows_dev - own_w - 1), (0, 0)))
    mine = lax.psum_scatter(
        give.reshape(everyone * back_rows_dev, shared_width), ("dp", "tensor"), scatter_dimension=0, tiled=True
    )
    owned_shared, own_row = mine[:own_w], mine[own_w]
    owned_pre = own_row[:own_g]
    owned_kernel = own_row[own_g : own_g + own_c * taps].reshape(own_c, taps)
    owned_bias = own_row[own_g + own_c * taps : own_g + own_c * taps + own_c]

    heads_row = jnp.concatenate([jnp.sum(d_step, axis=0), d_decay])
    heads_row = jnp.pad(heads_row, (0, inner - 2 * heads))[None, :]
    sums_dp = lax.psum(jnp.concatenate([acc_inner[:7], heads_row], axis=0), "dp")
    return (
        output,
        grad_tokens,
        owned_pre,
        owned_split[:, :inner],
        owned_split[:, inner : 2 * inner],
        owned_shared,
        owned_split[:, 2 * inner : 2 * inner + heads],
        sums_dp[:4].T,
        sums_dp[4],
        owned_kernel,
        owned_bias,
        sums_dp[7, :heads],
        sums_dp[7, heads : 2 * heads],
        sums_dp[5].reshape(heads, head_width).sum(axis=1),
        sums_dp[6],
        owned_out,
    )

def solution(mesh):
    in_specs = (
        P(("dp", "tensor"), None),
        P("dp", None),
        P(("dp", "tensor"), None),
        P(("dp", "tensor")),
        P("dp", "tensor"),
        P("dp", "tensor"),
        P(("dp", "tensor"), None),
        P("dp", "tensor"),
        P("tensor", None),
        P("tensor"),
        P(("dp", "tensor"), None),
        P(("dp", "tensor")),
        P("tensor"),
        P("tensor"),
        P("tensor"),
        P("tensor"),
        P("tensor", "dp"),
    )
    out_specs = (
        P(("dp", "tensor"), None),
        P(("dp", "tensor"), None),
        P(("dp", "tensor")),
        P("dp", "tensor"),
        P("dp", "tensor"),
        P(("dp", "tensor"), None),
        P("dp", "tensor"),
        P("tensor", None),
        P("tensor"),
        P(("dp", "tensor"), None),
        P(("dp", "tensor")),
        P("tensor"),
        P("tensor"),
        P("tensor"),
        P("tensor"),
        P("tensor", "dp"),
    )
    return jax.shard_map(shards, mesh=mesh, in_specs=in_specs, out_specs=out_specs, check_vma=False)
```

```python
import functools

import jax
import jax.numpy as jnp
from jax import lax
from jax.experimental import pallas as pl
from jax.experimental.pallas import tpu as pltpu
from jax.sharding import PartitionSpec as P

EPS = 1e-05
HIGH = lax.Precision.HIGHEST
Q = 128
LANES = 128
F32 = jnp.float32
BF16 = jnp.bfloat16
LAST = (((1,), (1,)), ((), ()))
FIRST = (((0,), (0,)), ((), ()))
VMEM_LIMIT = 56 * 1024 * 1024


def segment_ids(lengths, count):
    ends = jnp.cumsum(lengths)
    places = lax.broadcasted_iota(jnp.int32, (count, ends.shape[0]), 0)
    return jnp.sum((places >= ends[None, :]).astype(jnp.int32), axis=1)


def contract_last(left, right):
    return lax.dot_general(left, right, LAST, preferred_element_type=F32)


def contract_first(left, right):
    return lax.dot_general(left, right, FIRST, preferred_element_type=F32)


def mul(left, right):
    return jnp.dot(left, right, preferred_element_type=F32)


def halves(value):
    high = value.astype(BF16)
    return high, (value - high.astype(F32)).astype(BF16)


def spread(value, expand):
    high, low = halves(value)
    return mul(high, expand) + mul(low, expand)


def per_head(value, expand):
    high, low = halves(value)
    return contract_last(high, expand) + contract_last(low, expand)


def shifted(value, halo, cols):
    ext = jnp.concatenate([halo, value], axis=0)
    return [pltpu.roll(ext, s, axis=0)[8:] * cols[:, s : s + 1] for s in (1, 2, 3)]


def convolve(value, earlier, taps):
    total = taps[4:5] + taps[3:4] * value
    for s in (1, 2, 3):
        total = total + taps[3 - s : 4 - s] * earlier[s - 1]
    return total


def convolve_back(grad, later, cols, taps):
    ext = jnp.concatenate([grad, later], axis=0)
    count = grad.shape[0]
    total = taps[3:4] * grad
    for s in (1, 2, 3):
        moved = pltpu.roll(ext, count + 8 - s, axis=0)[:count]
        total = total + taps[3 - s : 4 - s] * (moved * cols[:, 5 + s : 6 + s])
    return total


def tap_grads(grad, value, earlier):
    rows = [jnp.sum(grad * earlier[2 - k], axis=0, keepdims=True) for k in range(3)]
    rows.append(jnp.sum(grad * value, axis=0, keepdims=True))
    rows.append(jnp.sum(grad, axis=0, keepdims=True))
    return rows


def block_terms(pre_ref, halo_ref, sh_ref, halo_sh_ref, step_ref, rate_ref, rate_row_ref, cols, seg_row_ref, ti, ts, expand):
    pre, sh = pre_ref[...], sh_ref[...]
    near, near_s = shifted(pre, halo_ref[...], cols), shifted(sh, halo_sh_ref[...], cols)
    z, zs = convolve(pre, near, ti), convolve(sh, near_s, ts)
    rows = lax.broadcasted_iota(jnp.int32, (Q, Q), 0)
    lanes = lax.broadcasted_iota(jnp.int32, (Q, Q), 1)
    lower = (rows >= lanes).astype(F32)
    upper = (rows <= lanes).astype(F32)
    logs = jnp.dot(lower, rate_ref[...], precision=HIGH, preferred_element_type=F32)
    logs_row = jnp.dot(rate_row_ref[...], upper, precision=HIGH, preferred_element_type=F32)
    step_e = spread(step_ref[...], expand)
    carried = spread(jnp.exp(logs) * cols[:, 4:5], expand)
    tail = spread(jnp.exp(logs[Q - 1 : Q] - logs) * cols[:, 5:6], expand)
    mask = (cols[:, 0:1] == seg_row_ref[0:1, :]) & (rows >= lanes)
    return pre, sh, near, near_s, z, zs, logs, logs_row, step_e, carried, tail, mask


def decays(logs, logs_row, mask, h):
    diff = logs[:, h : h + 1] - logs_row[h : h + 1, :]
    return jnp.exp(jnp.where(mask, diff, -10000.0))


def forward_kernel(
    heads, pre_ref, halo_ref, gate_ref, sh_ref, halo_sh_ref, step_ref, rate_ref, rate_row_ref,
    cols_ref, seg_row_ref, ti_ref, ts_ref, expand_ref, gated_ref, states_ref, sums_ref, state,
):
    @pl.when(pl.program_id(0) == 0)
    def _():
        state[...] = jnp.zeros_like(state)

    cols, ti, ts, expand = cols_ref[...], ti_ref[...], ts_ref[...], expand_ref[...]
    _, _, _, _, z, zs, logs, logs_row, step_e, carried, tail, mask = block_terms(
        pre_ref, halo_ref, sh_ref, halo_sh_ref, step_ref, rate_ref, rate_row_ref, cols, seg_row_ref, ti, ts, expand
    )
    x = z * jax.nn.sigmoid(z)
    shared = (zs * jax.nn.sigmoid(zs)).astype(BF16)
    b, c = shared[:, :LANES], shared[:, LANES:]
    xs = step_e * x
    low_lanes = ti[7:8]
    x_even = (xs * low_lanes).astype(BF16)
    x_odd = (xs * (1.0 - low_lanes)).astype(BF16)
    entering = state[...]
    entering_low = entering.astype(BF16)
    states_ref[...] = entering_low
    scores = contract_last(c, b)
    base = carried * mul(c, entering_low) + ti[5:6] * x
    state[...] = carried[Q - 1 : Q] * entering + contract_first(b, (tail * xs).astype(BF16))
    total = jnp.zeros((Q, LANES), F32)
    for pair in range(heads // 2):
        at = slice(pair * LANES, (pair + 1) * LANES)
        both = jnp.concatenate(
            [scores * decays(logs, logs_row, mask, 2 * pair + i) for i in range(2)], axis=1
        ).astype(BF16)
        y = base[:, at] + mul(both, jnp.concatenate([x_even[:, at], x_odd[:, at]], axis=0))
        gate = gate_ref[:, at]
        gated = y * (gate * jax.nn.sigmoid(gate))
        gated_ref[:, at] = gated
        total = total + gated * gated
    sums_ref[...] = jnp.broadcast_to(jnp.sum(total, axis=1, keepdims=True), (Q, LANES))


def backward_kernel(
    heads, pre_ref, halo_ref, gate_ref, sh_ref, halo_sh_ref, step_ref, rate_ref, rate_row_ref,
    cols_ref, seg_row_ref, ti_ref, ts_ref, expand_ref, states_ref, gm_ref, gated_ref, norms_ref,
    low_ref, dsh_ref, dstep_ref, dlog_ref, dlog_row_ref, acc_i_ref, acc_s_ref,
    dstate, later, later_s,
):
    @pl.when(pl.program_id(0) == 0)
    def _():
        dstate[...] = jnp.zeros_like(dstate)
        later[...] = jnp.zeros_like(later)
        later_s[...] = jnp.zeros_like(later_s)
        acc_i_ref[...] = jnp.zeros_like(acc_i_ref)
        acc_s_ref[...] = jnp.zeros_like(acc_s_ref)

    width = pre_ref.shape[1]
    cols, ti, ts, expand = cols_ref[...], ti_ref[...], ts_ref[...], expand_ref[...]
    pre, sh, near, near_s, z, zs, logs, logs_row, step_e, carried, tail, mask = block_terms(
        pre_ref, halo_ref, sh_ref, halo_sh_ref, step_ref, rate_ref, rate_row_ref, cols, seg_row_ref, ti, ts, expand
    )
    sig, sig_s = jax.nn.sigmoid(z), jax.nn.sigmoid(zs)
    x = z * sig
    shared = (zs * sig_s).astype(BF16)
    b, c = shared[:, :LANES], shared[:, LANES:]
    xs = step_e * x
    low_lanes = ti[7:8]
    high_lanes = 1.0 - low_lanes
    x_low = xs.astype(BF16)
    x_even = (xs * low_lanes).astype(BF16)
    x_odd = (xs * high_lanes).astype(BF16)
    skip = ti[5:6]

    gm, gated, gate, norms = gm_ref[...], gated_ref[...], gate_ref[...], norms_ref[...]
    rmix, pull = norms[:, 0:1], norms[:, 1:2]
    dgated = gm * ti[6:7] * rmix - gated * pull
    dgain = jnp.sum(gm * gated * rmix, axis=0, keepdims=True)
    sig_g = jax.nn.sigmoid(gate)
    dy = dgated * (gate * sig_g)
    dgate_scale = dgated * (sig_g * (1.0 + gate * (1.0 - sig_g)))
    dy_even = (dy * low_lanes).astype(BF16)
    dy_odd = (dy * high_lanes).astype(BF16)

    entering = states_ref[...]
    leaving = dstate[...]
    leaving_low = leaving.astype(BF16)
    scores = contract_last(c, b)
    from_state = carried * mul(c, entering)
    base = from_state + skip * x
    carried_dy = carried * dy
    carried_low = carried_dy.astype(BF16)
    tail_x = tail * xs
    tail_low = tail_x.astype(BF16)
    reach = mul(b, leaving_low)
    last_row = carried[Q - 1 : Q]
    pulled = jnp.sum(entering.astype(F32) * leaving, axis=0, keepdims=True) * last_row
    dstate[...] = last_row * leaving + contract_first(c, carried_low)

    lane = lax.broadcasted_iota(jnp.int32, (Q, LANES), 1)
    dscores = jnp.zeros((Q, Q), F32)
    row_sums = jnp.zeros((Q, LANES), F32)
    col_sums = []
    grads = []
    for pair in range(heads // 2):
        at = slice(pair * LANES, (pair + 1) * LANES)
        weights = [decays(logs, logs_row, mask, 2 * pair + i) for i in range(2)]
        mats = [(scores * w).astype(BF16) for w in weights]
        y = base[:, at] + mul(
            jnp.concatenate(mats, axis=1), jnp.concatenate([x_even[:, at], x_odd[:, at]], axis=0)
        )
        low_ref[:, at] = (dgate_scale[:, at] * y).astype(BF16)
        dys = jnp.concatenate([dy_even[:, at], dy_odd[:, at]], axis=0)
        cross = contract_last(dys, x_low[:, at])
        for i in range(2):
            part = cross[i * Q : (i + 1) * Q] * weights[i]
            dscores = dscores + part
            part = part * scores
            h = 2 * pair + i
            row_sums = jnp.where(lane == h, jnp.sum(part, axis=1, keepdims=True), row_sums)
            col_sums.append(jnp.sum(part, axis=0, keepdims=True))
        grads.append(contract_first(jnp.concatenate(mats, axis=0), dys))
    spare = dlog_row_ref.shape[0] - heads
    if spare:
        col_sums.append(jnp.zeros((spare, Q), F32))
    dlog_row_ref[...] = jnp.concatenate(col_sums, axis=0)
    dxs = jnp.concatenate(grads, axis=1) + tail * reach

    tail_term = tail_x * reach
    at_end = pulled + jnp.sum(tail_term, axis=0, keepdims=True)
    ends = lax.broadcasted_iota(jnp.int32, (Q, width), 0) == Q - 1
    log_term = dy * from_state - tail_term + jnp.where(ends, at_end, 0.0)
    dlog_ref[...] = row_sums + per_head(log_term, expand)
    dstep_ref[...] = per_head(x * dxs, expand)

    dx = step_e * dxs + skip * dy
    dz = dx * (sig * (1.0 + z * (1.0 - sig)))
    low_ref[:, width:] = convolve_back(dz, later[...], cols, ti).astype(BF16)
    later[...] = dz[:8]
    rows = tap_grads(dz, pre, near)
    rows += [jnp.sum(dy * x, axis=0, keepdims=True), dgain, jnp.zeros((1, width), F32)]
    acc_i_ref[...] += jnp.concatenate(rows, axis=0)

    dlow = dscores.astype(BF16)
    dc = mul(dlow, b) + contract_last(carried_low, entering)
    db = contract_first(dlow, c) + contract_last(tail_low, leaving_low)
    dzs = jnp.concatenate([db, dc], axis=1) * (sig_s * (1.0 + zs * (1.0 - sig_s)))
    dsh_ref[...] = convolve_back(dzs, later_s[...], cols, ts)
    later_s[...] = dzs[:8]
    rows = tap_grads(dzs, sh, near_s) + [jnp.zeros((3, dzs.shape[1]), F32)]
    acc_s_ref[...] += jnp.concatenate(rows, axis=0)


def block_specs(width, shared_width, row_heads, blocks, place):
    def halo(k):
        return jnp.maximum(place(k) * (Q // 8) - 1, 0)

    return [
        pl.BlockSpec((Q, width), lambda k: (place(k), 1)),
        pl.BlockSpec((8, width), lambda k: (halo(k), 1)),
        pl.BlockSpec((Q, width), lambda k: (place(k), 0)),
        pl.BlockSpec((Q, shared_width), lambda k: (place(k), 0)),
        pl.BlockSpec((8, shared_width), lambda k: (halo(k), 0)),
        pl.BlockSpec((Q, LANES), lambda k: (place(k), 0)),
        pl.BlockSpec((Q, LANES), lambda k: (place(k), 0)),
        pl.BlockSpec((row_heads, Q), lambda k: (0, place(k))),
        pl.BlockSpec((Q, LANES), lambda k: (place(k), 0)),
        pl.BlockSpec((8, Q), lambda k: (0, place(k))),
        pl.BlockSpec((8, width), lambda k: (0, 0)),
        pl.BlockSpec((8, shared_width), lambda k: (0, 0)),
        pl.BlockSpec((LANES, width), lambda k: (0, 0)),
    ]


def mixer_forward(heads, width, args):
    proj, shared = args[0], args[3]
    count, shared_width, row_heads = proj.shape[0], shared.shape[1], args[7].shape[0]
    blocks = count // Q
    return pl.pallas_call(
        functools.partial(forward_kernel, heads),
        grid=(blocks,),
        in_specs=block_specs(width, shared_width, row_heads, blocks, lambda k: k),
        out_specs=[
            pl.BlockSpec((Q, width), lambda k: (k, 0)),
            pl.BlockSpec((LANES, width), lambda k: (k, 0)),
            pl.BlockSpec((Q, LANES), lambda k: (k, 0)),
        ],
        out_shape=[
            jax.ShapeDtypeStruct((count, width), F32),
            jax.ShapeDtypeStruct((blocks * LANES, width), BF16),
            jax.ShapeDtypeStruct((count, LANES), F32),
        ],
        scratch_shapes=[pltpu.VMEM((LANES, width), F32)],
        compiler_params=pltpu.CompilerParams(vmem_limit_bytes=VMEM_LIMIT),
        cost_estimate=pl.CostEstimate(flops=count * width * 1500, bytes_accessed=count * width * 14, transcendentals=count * width * 4),
    )(*args)


def mixer_backward(heads, width, args):
    proj, shared = args[0], args[3]
    count, shared_width, row_heads = proj.shape[0], shared.shape[1], args[7].shape[0]
    blocks = count // Q
    here = lambda k: blocks - 1 - k
    rows = lambda k: (here(k), 0)
    return pl.pallas_call(
        functools.partial(backward_kernel, heads),
        grid=(blocks,),
        in_specs=block_specs(width, shared_width, row_heads, blocks, here)
        + [
            pl.BlockSpec((LANES, width), rows),
            pl.BlockSpec((Q, width), rows),
            pl.BlockSpec((Q, width), rows),
            pl.BlockSpec((Q, LANES), rows),
        ],
        out_specs=[
            pl.BlockSpec((Q, 2 * width), rows),
            pl.BlockSpec((Q, shared_width), rows),
            pl.BlockSpec((Q, LANES), rows),
            pl.BlockSpec((Q, LANES), rows),
            pl.BlockSpec((row_heads, Q), lambda k: (0, here(k))),
            pl.BlockSpec((8, width), lambda k: (0, 0)),
            pl.BlockSpec((8, shared_width), lambda k: (0, 0)),
        ],
        out_shape=[
            jax.ShapeDtypeStruct((count, 2 * width), BF16),
            jax.ShapeDtypeStruct((count, shared_width), F32),
            jax.ShapeDtypeStruct((count, LANES), F32),
            jax.ShapeDtypeStruct((count, LANES), F32),
            jax.ShapeDtypeStruct((row_heads, count), F32),
            jax.ShapeDtypeStruct((8, width), F32),
            jax.ShapeDtypeStruct((8, shared_width), F32),
        ],
        scratch_shapes=[
            pltpu.VMEM((LANES, width), F32),
            pltpu.VMEM((8, width), F32),
            pltpu.VMEM((8, shared_width), F32),
        ],
        compiler_params=pltpu.CompilerParams(vmem_limit_bytes=VMEM_LIMIT),
        cost_estimate=pl.CostEstimate(flops=count * width * 4000, bytes_accessed=count * width * 24, transcendentals=count * width * 5),
    )(*args)


def pad_lanes(value, lanes=LANES):
    return jnp.pad(value, ((0, 0), (0, lanes - value.shape[1])))


def token_columns(seg, heads):
    count = seg.shape[0]
    early = [jnp.concatenate([jnp.full((s,), -1, jnp.int32), seg[:-s]]) == seg for s in (1, 2, 3)]
    late = [jnp.concatenate([seg[s:], jnp.full((s,), -1, jnp.int32)]) == seg for s in (1, 2, 3)]
    by_block = seg.reshape(count // Q, Q)
    prev = jnp.concatenate([jnp.full((1,), -1, jnp.int32), by_block[:-1, -1]])
    enters = (by_block == prev[:, None]).reshape(count)
    leaves = (by_block == by_block[:, -1:]).reshape(count)
    stack = [seg] + early + [enters, leaves] + late
    return pad_lanes(jnp.stack([v.astype(F32) for v in stack], axis=1))


def shards(
    tokens, lengths, cotangent, pre_gain, w_gate, w_inner, w_shared, w_step, conv_inner,
    conv_inner_bias, conv_shared, conv_shared_bias, step_bias, decay_log, skip_gain, mix_gain, w_out,
):
    tensor_count, dp_count = lax.axis_size("tensor"), lax.axis_size("dp")
    everyone = tensor_count * dp_count
    rows_dev, width = tokens.shape
    group = rows_dev * tensor_count
    heads = step_bias.shape[0]
    inner = w_gate.shape[1]
    head_width = inner // heads
    shared_width = w_shared.shape[1]
    inner_all = inner * tensor_count
    row_heads = -(-heads // 8) * 8

    own_w, own_g, own_c = w_shared.shape[0], pre_gain.shape[0], conv_shared.shape[0]
    taps = conv_shared.shape[1]
    extra = jnp.concatenate([pre_gain, conv_shared.reshape(-1), conv_shared_bias])
    extra = jnp.pad(extra, (0, shared_width - extra.shape[0]))[None, :]
    packed_rows = -(-(own_w + 1) // 16) * 16
    packed = jnp.concatenate([w_shared, extra], axis=0)
    packed = jnp.pad(packed, ((0, packed_rows - own_w - 1), (0, 0)))
    packed = lax.all_gather(lax.all_gather(packed, "tensor", axis=0, tiled=True), "dp", axis=0, tiled=True)
    packed = packed.reshape(everyone, packed_rows, shared_width)
    shared_full = packed[:, :own_w].reshape(width, shared_width)
    extras = packed[:, own_w]
    gain_full = extras[:, :own_g].reshape(-1)
    kernel_shared = extras[:, own_g : own_g + own_c * taps].reshape(shared_width, taps)
    bias_shared = extras[:, own_g + own_c * taps : own_g + own_c * taps + own_c].reshape(-1)

    split_full = lax.all_gather(
        jnp.concatenate([w_gate, w_inner, pad_lanes(w_step)], axis=1), "dp", axis=0, tiled=True
    )
    out_full = lax.all_gather(w_out.T, "dp", axis=0, tiled=True)
    cot_all = lax.all_gather(cotangent, "tensor", axis=0, tiled=True)

    rows = tokens.astype(F32)
    gain_pre = gain_full.astype(F32)[None, :]
    rinv = lax.rsqrt(jnp.mean(rows * rows, axis=-1, keepdims=True) + EPS)
    normed_in = (rows * rinv * gain_pre).astype(BF16)
    rows_all = lax.all_gather(tokens, "tensor", axis=0, tiled=True).astype(F32)
    rinv_all = lax.rsqrt(jnp.mean(rows_all * rows_all, axis=-1, keepdims=True) + EPS)
    gathered = (rows_all * rinv_all * gain_pre).astype(BF16)
    proj = mul(gathered, split_full[:, : 2 * inner])
    step_raw = mul(gathered, split_full[:, 2 * inner :])[:, :heads]
    shared_pre = mul(gathered, shared_full)
    seg = segment_ids(lengths[0], group)

    shifted_step = step_raw + step_bias[None, :]
    step = jax.nn.softplus(shifted_step)
    decay = -jnp.exp(decay_log)
    rate = step * decay[None, :]
    rate_row = jnp.pad(rate.T, ((0, row_heads - heads), (0, 0)))
    cols = token_columns(seg, heads)
    seg_row = jnp.broadcast_to(seg.astype(F32)[None, :], (8, group))
    channel = jnp.arange(inner)
    low_lanes = (channel % LANES < head_width).astype(F32)
    gain_mix = mix_gain.astype(F32)
    taps_inner = jnp.concatenate(
        [conv_inner.T, jnp.stack([conv_inner_bias, jnp.repeat(skip_gain, head_width), gain_mix, low_lanes])]
    )
    taps_shared = jnp.pad(
        jnp.concatenate([kernel_shared.T, bias_shared[None, :]]).astype(F32), ((0, 7 - taps), (0, 0))
    )
    expand = (jnp.arange(LANES)[:, None] == channel[None, :] // head_width).astype(BF16)
    args = (
        proj, proj, proj, shared_pre, shared_pre, pad_lanes(step), pad_lanes(rate), rate_row,
        cols, seg_row, taps_inner, taps_shared, expand,
    )
    gated, states, sums = mixer_forward(heads, inner, args)

    grad_mixed = mul(cot_all, out_full)
    crosses = jnp.sum(grad_mixed * gain_mix[None, :] * gated, axis=-1)
    square_sum, cross = lax.psum(jnp.stack([sums[:, 0], crosses]), "tensor")
    rmix = lax.rsqrt(square_sum / inner_all + EPS)
    mixed = (gated * rmix[:, None] * gain_mix[None, :]).astype(BF16)
    out_term = contract_first(cot_all, mixed).astype(BF16)
    partial_value = contract_last(mixed, out_full)
    rmix, cross, partial_value, out_term = lax.optimization_barrier((rmix, cross, partial_value, out_term))
    out_rows = lax.psum_scatter(partial_value, "tensor", scatter_dimension=0, tiled=True)
    owned_out = lax.psum_scatter(out_term, "dp", scatter_dimension=0, tiled=True).astype(F32).T
    output = (rows + out_rows).astype(BF16)

    norms = pad_lanes(jnp.stack([rmix, rmix**3 * cross / inner_all], axis=1))
    low, d_shared, d_step_part, d_log, d_log_row, acc_inner, acc_shared = mixer_backward(
        heads, inner, args + (states, grad_mixed, gated, norms)
    )
    d_logs = (d_log[:, :heads] - d_log_row[:heads].T).reshape(group // Q, Q, heads)
    after = (jnp.arange(Q)[:, None] <= jnp.arange(Q)[None, :]).astype(F32)
    d_rate = jnp.einsum("ti,kih->kth", after, d_logs, precision=HIGH).reshape(group, heads)
    d_step = (d_step_part[:, :heads] + d_rate * decay[None, :]) * jax.nn.sigmoid(shifted_step)
    d_decay = jnp.sum(d_rate * step, axis=0) * decay
    step_low = pad_lanes(d_step.astype(BF16))

    back_part = contract_last(low, split_full[:, : 2 * inner]) + contract_last(
        step_low, split_full[:, 2 * inner :]
    )
    split_grad = jnp.concatenate(
        [contract_first(gathered, low).astype(BF16), contract_first(gathered, step_low).astype(BF16)], axis=1
    )
    owned_split = lax.psum_scatter(split_grad, "dp", scatter_dimension=0, tiled=True).astype(F32)
    back_rows = lax.psum_scatter(
        jnp.concatenate([back_part, d_shared], axis=1), "tensor", scatter_dimension=0, tiled=True
    )
    shared_low = back_rows[:, width:].astype(BF16)
    back_rows = back_rows[:, :width] + contract_last(shared_low, shared_full)
    grad_shared_w = contract_first(normed_in, shared_low)
    grad_pre = jnp.sum(back_rows * rows * rinv, axis=0)
    upstream_pre = back_rows * gain_pre
    grad_tokens = (
        upstream_pre * rinv
        - rows * rinv**3 * jnp.sum(upstream_pre * rows, axis=-1, keepdims=True) / width
        + cotangent.astype(F32)
    )
    tail = jnp.concatenate(
        [
            grad_pre.reshape(everyone, own_g),
            acc_shared[:taps].T.reshape(everyone, own_c * taps),
            acc_shared[taps].reshape(everyone, own_c),
        ],
        axis=1,
    )
    tail = pad_lanes(tail, shared_width)[:, None, :]
    back_rows_dev = -(-(own_w + 1) // 8) * 8
    give = jnp.concatenate([grad_shared_w.reshape(everyone, own_w, shared_width), tail], axis=1)
    give = jnp.pad(give, ((0, 0), (0, back_rows_dev - own_w - 1), (0, 0)))
    mine = lax.psum_scatter(
        give.reshape(everyone * back_rows_dev, shared_width), "dp", scatter_dimension=0, tiled=True
    )
    mine = lax.psum_scatter(mine, "tensor", scatter_dimension=0, tiled=True)
    owned_shared, own_row = mine[:own_w], mine[own_w]
    owned_pre = own_row[:own_g]
    owned_kernel = own_row[own_g : own_g + own_c * taps].reshape(own_c, taps)
    owned_bias = own_row[own_g + own_c * taps : own_g + own_c * taps + own_c]

    heads_row = jnp.concatenate([jnp.sum(d_step, axis=0), d_decay])
    heads_row = jnp.pad(heads_row, (0, inner - 2 * heads))[None, :]
    own_sums = jnp.concatenate([acc_inner[:7], heads_row], axis=0)
    sums_dp = jnp.sum(lax.all_gather(own_sums, "dp", axis=0, tiled=True).reshape(dp_count, 8, inner), axis=0)
    return (
        output,
        grad_tokens,
        owned_pre,
        owned_split[:, :inner],
        owned_split[:, inner : 2 * inner],
        owned_shared,
        owned_split[:, 2 * inner : 2 * inner + heads],
        sums_dp[:4].T,
        sums_dp[4],
        owned_kernel,
        owned_bias,
        sums_dp[7, :heads],
        sums_dp[7, heads : 2 * heads],
        sums_dp[5].reshape(heads, head_width).sum(axis=1),
        sums_dp[6],
        owned_out,
    )

def solution(mesh):
    in_specs = (
        P(("dp", "tensor"), None),
        P("dp", None),
        P(("dp", "tensor"), None),
        P(("dp", "tensor")),
        P("dp", "tensor"),
        P("dp", "tensor"),
        P(("dp", "tensor"), None),
        P("dp", "tensor"),
        P("tensor", None),
        P("tensor"),
        P(("dp", "tensor"), None),
        P(("dp", "tensor")),
        P("tensor"),
        P("tensor"),
        P("tensor"),
        P("tensor"),
        P("tensor", "dp"),
    )
    out_specs = (
        P(("dp", "tensor"), None),
        P(("dp", "tensor"), None),
        P(("dp", "tensor")),
        P("dp", "tensor"),
        P("dp", "tensor"),
        P(("dp", "tensor"), None),
        P("dp", "tensor"),
        P("tensor", None),
        P("tensor"),
        P(("dp", "tensor"), None),
        P(("dp", "tensor")),
        P("tensor"),
        P("tensor"),
        P("tensor"),
        P("tensor"),
        P("tensor", "dp"),
    )
    return jax.shard_map(shards, mesh=mesh, in_specs=in_specs, out_specs=out_specs, check_vma=False)
```
